256 devices in a mesh: dp: 16 (over x_lo, z), row: 4 (over y), col: 4 (over x_hi, core).
Axes of the slice: x: 4 (x_hi: 2, x_lo: 2; x = x_hi * 2 + x_lo), y: 4, z: 8, core: 2. Of those that a mesh axis runs over, the one named last changes fastest.
Arguments:
- tokens: bfloat16 [32768, 6144], P(('dp', 'row'), 'col'), parts along dimension 0, may hold values from -6 to 6
- w_up: bfloat16 [6144, 3072], P('row', 'col'), may hold values from -0.078125 to 0.078125
- cotangent: bfloat16 [32768, 3072], P(('dp', 'row'), 'col'), parts along dimension 0, may hold values from -6 to 6
Outputs:
- hidden: bfloat16 [32768, 3072], P(('dp', 'row'), 'col'), parts along dimension 0
- d_tokens: bfloat16 [32768, 6144], P(('dp', 'col'), 'row'), parts along dimension 0
The draws below stay inside these ranges and needn't reach their ends.
There are 16 independent parts, one for each index of `dp`. The reference program is written for one: setup_inputs(seed, part) draws one part's arguments, and reference() takes and returns one part's arrays. A program takes and returns all parts, laid end to end along the dimension named above; an argument that names none is the same for every part. Nothing has to cross between parts.
All inputs are finite; a program needn't handle non-finite values.
Results may differ from the reference program's by a relative error of at most 0.0049.
Values may be sent and summed in bfloat16 or wider, within the bound.
No kernel may reach another device: no remote copies, remote signals or barrier semaphores. Data moves between devices by JAX's collectives and lax.ppermute only.
A program may use at most 128 MiB of HBM per device.

```python
import math
import jax
import jax.numpy as jnp
from jax import lax

D = 6144
FF = 3072
TOKENS = 2048


def block_levels(rng, dims, pieces, smallest, high):
    loudness, own = 1.0, jax.random.fold_in(rng, 6)
    for dim, shards_of in pieces:
        steps = jnp.exp(jax.random.uniform(jax.random.fold_in(own, dim), (shards_of,), jnp.float32, smallest / len(pieces), high / len(pieces)))
        loudness = loudness * jnp.repeat(steps, dims[dim] // shards_of).reshape([-1 if axis == dim else 1 for axis in range(len(dims))])
    return loudness


def normal_values(key, shape, width, bound, shards=(), kind=jnp.bfloat16):
    entries = jax.random.normal(key, shape, jnp.float32) * width
    if len(shards) > 0:
        entries = block_levels(key, shape, shards, -0.22, 0.18) * entries
    return jnp.clip(entries, min=-bound, max=bound).astype(kind)


def setup_inputs(seed: int = 0, part: int = 0) -> dict:
    seeds = jax.random.split(jax.random.key(seed), 4)
    part_keys = jax.random.split(jax.random.fold_in(seeds[3], part), 4)
    tokens = normal_values(part_keys[0], (TOKENS, D), 1.0, 6.0, ((0, 4), (1, 4)))
    w_up = normal_values(seeds[1], (D, FF), D ** -0.5, 0.078125, ((0, 4), (1, 4)))
    cotangent = normal_values(part_keys[2], (TOKENS, FF), 1.0, 6.0, ((0, 4), (1, 4)))
    return {"tokens": tokens, "w_up": w_up, "cotangent": cotangent}


coeff = math.sqrt(2.0 / math.pi)

def reference(tokens, w_up, cotangent):
    pre = jnp.dot(tokens, w_up, preferred_element_type=jnp.float32)
    inner = coeff * (pre + 0.044715 * pre * pre * pre)
    tanh_val = jnp.tanh(inner)
    hidden = (0.5 * pre * (1.0 + tanh_val)).astype(jnp.bfloat16)
    slope = 0.5 * (1.0 + tanh_val) + 0.5 * pre * (1.0 - tanh_val * tanh_val) * coeff * (1.0 + 3.0 * 0.044715 * pre * pre)
    d_pre = (cotangent.astype(jnp.float32) * slope).astype(jnp.bfloat16)
    d_tokens = lax.dot_general(d_pre, w_up, (((1,), (1,)), ((), ())), preferred_element_type=jnp.float32)
    return (hidden, d_tokens.astype(jnp.bfloat16))
```

```python
import functools
import math

import jax
import jax.numpy as jnp
from jax import lax
from jax.experimental import pallas as pl
from jax.experimental.pallas import tpu as pltpu
from jax.sharding import PartitionSpec as P

COEFF = math.sqrt(2.0 / math.pi)
MIB = 1 << 20


def route(sizes, target):
    pairs = []
    for i in range(sizes[0]):
        for j in range(sizes[1]):
            a, b = target(i, j)
            pairs.append((i * sizes[1] + j, a * sizes[1] + b))
    return pairs


def to_row(x, d):
    n = lax.axis_size("row")
    return lax.ppermute(x, "row", [(i, (i + d) % n) for i in range(n)])


def col_swap(x, m):
    n = lax.axis_size("col")
    return lax.ppermute(x, "col", [(i, i ^ m) for i in range(n)])


def turned(r, c):
    core = c & 1
    if (c >> 1) != (r >> 1):
        step = 2 if core else 0
    else:
        step = 1 if core else -1
    return (r + step) % 4, r


def mirror(x):
    return lax.ppermute(x, ("row", "col"), route((4, 4), turned))


def turned_from(row, col):
    step = (row - col + 4) & 3
    cross = 1 - (step & 1)
    core = jnp.where((step == 1) | (step == 2), 1, 0)
    return 2 * ((col >> 1) ^ cross) + core


def ring(x):
    h = x.shape[0] // 2
    prev, nxt = to_row(x, 1), to_row(x, -1)
    return prev, nxt, to_row(prev[:h], 1), to_row(nxt[h:], -1)


def z_gather(x):
    dp = lax.axis_size("dp")
    z = min(8, dp)
    groups = [list(range(i, i + z)) for i in range(0, dp, z)]
    return lax.all_gather(x, "dp", axis_index_groups=groups)


def gelu_parts(pre):
    sq = pre * pre
    t = jnp.tanh(COEFF * (pre + 0.044715 * sq * pre))
    hidden = 0.5 * pre * (1.0 + t)
    slope = 0.5 * (1.0 + t) + 0.5 * pre * (1.0 - t * t) * COEFF * (1.0 + 3.0 * 0.044715 * sq)
    return hidden, slope


def up_kernel(at, nw, t0, t1, t2, t3, *rest):
    w_refs = rest[:nw]
    cot, hidden, d_pre, t_buf, w_buf, c_buf, acc, t_sem, w_sem, c_sem = rest[nw:]
    r, c = lax.axis_index("row"), lax.axis_index("col")
    for m, src in enumerate((t0, t1, t2, t3)):
        slot = c ^ m
        pltpu.make_async_copy(src, t_buf.at[slot], t_sem.at[slot]).start()
    if nw == 5:
        own, prev, nxt, far_a, far_b = w_refs
        h = far_a.shape[0]
        width = w_buf.shape[2]
        a, b, d, e = r, (r + 3) & 3, (r + 1) & 3, (r + 2) & 3
        pltpu.make_async_copy(own.at[:, pl.ds(at, width)], w_buf.at[a], w_sem.at[a]).start()
        pltpu.make_async_copy(prev, w_buf.at[b], w_sem.at[b]).start()
        pltpu.make_async_copy(nxt, w_buf.at[d], w_sem.at[d]).start()
        pltpu.make_async_copy(far_a, w_buf.at[e, pl.ds(0, h)], w_sem.at[e]).start()
        pltpu.make_async_copy(far_b, w_buf.at[e, pl.ds(h, h)], w_sem.at[e]).start()
    else:
        own, gathered = w_refs
        width = w_buf.shape[2]
        zs, _, part, _ = gathered.shape
        pltpu.make_async_copy(own.at[:, pl.ds(at, width)], w_buf.at[r], w_sem.at[r]).start()
        for i, d in enumerate((3, 1, 2)):
            slot = (r + d) & 3
            for z in range(zs):
                pltpu.make_async_copy(
                    gathered.at[z, i], w_buf.at[slot, pl.ds(z * part, part)], w_sem.at[slot]
                ).start()
    c_copy = pltpu.make_async_copy(cot.at[:, pl.ds(at, c_buf.shape[1])], c_buf, c_sem)
    c_copy.start()
    rows = t_buf.shape[1]
    tile = min(256, rows)
    for j in range(4):
        pltpu.make_async_copy(t0, t_buf.at[j], t_sem.at[j]).wait()
        pltpu.make_async_copy(own.at[:, pl.ds(at, w_buf.shape[2])], w_buf.at[j], w_sem.at[j]).wait()
        if j == 3:
            c_copy.wait()

        @pl.loop(0, rows // tile)
        def _(i):
            part_rows = pl.ds(pl.multiple_of(i * tile, tile), tile)
            y = jnp.dot(t_buf[j, part_rows, :], w_buf[j], preferred_element_type=jnp.float32)
            if j > 0:
                y = y + acc[part_rows, :]
            if j < 3:
                acc[part_rows, :] = y
            else:
                h_val, slope = gelu_parts(y)
                hidden[part_rows, :] = h_val.astype(hidden.dtype)
                d_pre[part_rows, :] = (c_buf[part_rows, :].astype(jnp.float32) * slope).astype(d_pre.dtype)


def up(tokens, w_pieces, cot, at, width):
    rows, depth = tokens[0].shape
    any_ = pl.BlockSpec(memory_space=pl.ANY)
    out = jax.ShapeDtypeStruct((rows, width), jnp.bfloat16)
    whole = pl.BlockSpec(memory_space=pltpu.VMEM)
    return pl.pallas_call(
        functools.partial(up_kernel, at, len(w_pieces)),
        out_shape=(out, out),
        in_specs=[any_] * (5 + len(w_pieces)),
        out_specs=(whole, whole),
        scratch_shapes=[
            pltpu.VMEM((4, rows, depth), jnp.bfloat16),
            pltpu.VMEM((4, depth, width), jnp.bfloat16),
            pltpu.VMEM((rows, width), jnp.bfloat16),
            pltpu.VMEM((rows, width), jnp.float32),
            pltpu.SemaphoreType.DMA((4,)),
            pltpu.SemaphoreType.DMA((4,)),
            pltpu.SemaphoreType.DMA,
        ],
        compiler_params=pltpu.CompilerParams(vmem_limit_bytes=28 * MIB),
        cost_estimate=pl.CostEstimate(
            flops=8 * rows * depth * width, bytes_accessed=8 * depth * (rows + width), transcendentals=rows * width
        ),
        name="up",
    )(*tokens, *w_pieces, cot)


def down_kernel(own, pair, x_part, z_part, x_pair, z_pair, *rest):
    pieces = rest[:10]
    out, g_buf, w_buf, g_sem, w_sem = rest[10:]
    r, c = lax.axis_index("row"), lax.axis_index("col")
    pltpu.make_async_copy(own, w_buf.at[c], w_sem.at[c]).start()
    pltpu.make_async_copy(pair, w_buf.at[c ^ 1], w_sem.at[c ^ 1]).start()
    h = x_part.shape[0]
    zs, part, _ = z_part.shape
    for m, xs, zp in ((2, x_part, z_part), (3, x_pair, z_pair)):
        slot = c ^ m
        pltpu.make_async_copy(xs, w_buf.at[slot, pl.ds(0, h)], w_sem.at[slot]).start()
        for z in range(zs):
            pltpu.make_async_copy(zp.at[z], w_buf.at[slot, pl.ds(h + z * part, part)], w_sem.at[slot]).start()
    width = pieces[0].shape[1]
    rows = pieces[0].shape[0]
    half = rows // 2
    for k in range(2):
        cols = pl.ds(k * width, width)
        mine, prev, nxt, far_a, far_b = pieces[5 * k : 5 * k + 5]
        for src, d in ((mine, 0), (prev, 3), (nxt, 1)):
            slot = turned_from((r + d) & 3, c)
            pltpu.make_async_copy(src, g_buf.at[slot, :, cols], g_sem.at[slot]).start()
        slot = turned_from((r + 2) & 3, c)
        pltpu.make_async_copy(far_a, g_buf.at[slot, pl.ds(0, half), cols], g_sem.at[slot]).start()
        pltpu.make_async_copy(far_b, g_buf.at[slot, pl.ds(half, half), cols], g_sem.at[slot]).start()
    for j in range(4):
        pltpu.make_async_copy(own, w_buf.at[j], w_sem.at[j]).wait()
        pltpu.make_async_copy(g_buf.at[j], g_buf.at[j], g_sem.at[j]).wait()
    depth = w_buf.shape[1]
    tile = 256

    @pl.loop(0, depth // tile)
    def _(i):
        at = pl.ds(pl.multiple_of(i * tile, tile), tile)
        total = None
        for j in range(4):
            y = lax.dot_general(
                g_buf[j], w_buf[j, at, :], (((1,), (1,)), ((), ())), preferred_element_type=jnp.float32
            )
            total = y if total is None else total + y
        out[:, at] = total.astype(out.dtype)


def down(w_pieces, pieces):
    depth, ff = w_pieces[0].shape
    rows = pieces[0].shape[0]
    any_ = pl.BlockSpec(memory_space=pl.ANY)
    return pl.pallas_call(
        down_kernel,
        out_shape=jax.ShapeDtypeStruct((rows, depth), jnp.bfloat16),
        in_specs=[any_] * 16,
        out_specs=pl.BlockSpec(memory_space=pltpu.VMEM),
        scratch_shapes=[
            pltpu.VMEM((4, rows, ff), jnp.bfloat16),
            pltpu.VMEM((4, depth, ff), jnp.bfloat16),
            pltpu.SemaphoreType.DMA((4,)),
            pltpu.SemaphoreType.DMA((4,)),
        ],
        compiler_params=pltpu.CompilerParams(vmem_limit_bytes=28 * MIB),
        cost_estimate=pl.CostEstimate(
            flops=8 * rows * depth * ff, bytes_accessed=8 * ff * (rows + depth), transcendentals=0
        ),
        name="down",
    )(*w_pieces, *pieces)


def body(tokens, w_up, cotangent):
    depth, ff = w_up.shape
    width = ff // 2
    zs = min(8, lax.axis_size("dp"))
    z = lax.axis_index("dp") % zs
    part = depth // zs
    piece = lax.dynamic_slice(w_up, (z * part, width), (part, width))
    slices = [to_row(piece, 1), to_row(piece, -1), to_row(piece, 2)]
    t_x = col_swap(tokens, 2)
    t_pair = col_swap(tokens, 1)
    late = z_gather(jnp.stack(slices))
    early = ring(w_up[:, :width])
    t_x_pair = col_swap(t_x, 1)
    ts = (tokens, t_pair, t_x, t_x_pair)
    half = depth // 2
    part2 = half // zs
    x_part = col_swap(w_up[:half], 2)
    piece2 = lax.dynamic_slice(w_up, (half + z * part2, 0), (part2, ff))
    z_part = z_gather(col_swap(piece2, 2))
    w_pair = col_swap(w_up, 1)
    x_pair = col_swap(x_part, 1)
    z_pair = col_swap(z_part, 1)

    hidden_a, d_a = up(ts, (w_up,) + early, cotangent, 0, width)
    m_a = mirror(d_a)
    g_a = (m_a,) + ring(m_a)
    hidden_b, d_b = up(ts, (w_up, late), cotangent, width, width)
    m_b = mirror(d_b)
    g_b = (m_b,) + ring(m_b)
    d_tokens = down((w_up, w_pair, x_part, z_part, x_pair, z_pair), g_a + g_b)
    return jnp.concatenate([hidden_a, hidden_b], axis=1), d_tokens


def solution(mesh):
    placed = (P(("dp", "row"), "col"), P("row", "col"), P(("dp", "row"), "col"))
    return jax.shard_map(
        body,
        mesh=mesh,
        in_specs=placed,
        out_specs=(P(("dp", "row"), "col"), P(("dp", "col"), "row")),
        check_vma=False,
    )
```

```python
import functools
import math

import jax
import jax.numpy as jnp
from jax import lax
from jax.experimental import pallas as pl
from jax.experimental.pallas import tpu as pltpu
from jax.sharding import PartitionSpec as P

COEFF = math.sqrt(2.0 / math.pi)
MIB = 1 << 20


ANY = pl.BlockSpec(memory_space=pl.ANY)
VMEM = pl.BlockSpec(memory_space=pltpu.VMEM)


def flat(sizes, target):
    pairs = []
    for i in range(sizes[0]):
        for j in range(sizes[1]):
            a, b = target(i, j)
            pairs.append((i * sizes[1] + j, a * sizes[1] + b))
    return pairs


def y_step(x, back=0):
    sizes = (lax.axis_size("row"), lax.axis_size("col"))
    return lax.ppermute(
        x, ("row", "col"), flat(sizes, lambda r, c: ((r + 1 - 2 * ((c ^ back) & 1)) % sizes[0], c))
    )


def z_size():
    return min(8, lax.axis_size("dp"))


def z_step(x, back=0):
    sizes, n = (lax.axis_size("dp"), lax.axis_size("col")), z_size()
    return lax.ppermute(
        x, ("dp", "col"), flat(sizes, lambda i, c: (i // n * n + (i % n + 1 - 2 * ((c ^ back) & 1)) % n, c))
    )


def opposite(x):
    n = lax.axis_size("row")
    return lax.ppermute(x, "row", [(i, (i + 2) % n) for i in range(n)])


def col_swap(x, m):
    n = lax.axis_size("col")
    return lax.ppermute(x, "col", [(i, i ^ m) for i in range(n)])


def turned(r, c):
    core = c & 1
    if (c >> 1) != (r >> 1):
        step = 2 if core else 0
    else:
        step = 1 if core else -1
    return (r + step) % 4, r


def mirror(x):
    return lax.ppermute(x, ("row", "col"), flat((4, 4), turned))


def turned_from(row, col):
    step = (row - col + 4) & 3
    cross = 1 - (step & 1)
    core = jnp.where((step == 1) | (step == 2), 1, 0)
    return 2 * ((col >> 1) ^ cross) + core


def away(i, s, core):
    return (i + jnp.where(core == 0, 4 - s, s)) & 3


def gelu_parts(pre):
    sq = pre * pre
    t = jnp.tanh(COEFF * (pre + 0.044715 * sq * pre))
    hidden = 0.5 * pre * (1.0 + t)
    slope = 0.5 * (1.0 + t) + 0.5 * pre * (1.0 - t * t) * COEFF * (1.0 + 3.0 * 0.044715 * sq)
    return hidden, slope


def params():
    return pltpu.CompilerParams(vmem_limit_bytes=16 * MIB)


def cost(flops, nbytes, trans=0):
    return pl.CostEstimate(flops=flops, bytes_accessed=nbytes, transcendentals=trans)


def mul(a, b):
    return jnp.dot(a, b, preferred_element_type=jnp.float32)


def sort_tokens_kernel(t0, t1, t2a, t2b, t3a, t3b, out, sem):
    c = lax.axis_index("col")
    h = t2a.shape[0]
    pltpu.make_async_copy(t0, out.at[c], sem).start()
    pltpu.make_async_copy(t1, out.at[c ^ 1], sem).start()
    for m, top, rest in ((2, t2a, t2b), (3, t3a, t3b)):
        pltpu.make_async_copy(top, out.at[c ^ m, pl.ds(0, h)], sem).start()
        pltpu.make_async_copy(rest, out.at[c ^ m, pl.ds(h, rest.shape[0])], sem).start()
    pltpu.make_async_copy(out, out, sem).wait()


def sort_tokens(*ts):
    rows, depth = ts[0].shape
    return pl.pallas_call(
        sort_tokens_kernel,
        out_shape=jax.ShapeDtypeStruct((4, rows, depth), jnp.bfloat16),
        in_specs=[ANY] * 6,
        out_specs=VMEM,
        scratch_shapes=[pltpu.SemaphoreType.DMA],
        compiler_params=params(),
        cost_estimate=cost(0, 16 * rows * depth),
        name="sort_tokens",
    )(*ts)


def up_part_kernel(t, own, w1, w3, p0, p1, p3, acc):
    r, core = lax.axis_index("row"), lax.axis_index("col") & 1
    z = lax.axis_index("dp") & 3
    _, q, width = p0.shape
    first, last = pl.ds(0, width), pl.ds(width, width)
    acc[...] = mul(t[r], own[...])
    for s, w in ((1, w1), (3, w3)):
        acc[:, first] += mul(t[away(r, s, core)], w[...])
    for s in range(1, 4):
        j = away(r, s, core)
        for u, p in ((0, p0), (1, p1), (3, p3)):
            k = pl.ds(pl.multiple_of(away(z, u, core) * q, 128), q)
            acc[:, last] += mul(t[j, :, k], p[s - 1])


def up_rest_kernel(t, so_far, w2, p2, cot, hidden, d_pre, acc):
    r, core = lax.axis_index("row"), lax.axis_index("col") & 1
    z = lax.axis_index("dp") & 3
    _, q, width = p2.shape
    first, last = pl.ds(0, width), pl.ds(width, width)
    acc[:, first] = so_far[:, first] + mul(t[away(r, 2, core)], w2[...])
    k = pl.ds(pl.multiple_of(away(z, 2, core) * q, 128), q)
    y = so_far[:, last]
    for s in range(1, 4):
        y += mul(t[away(r, s, core), :, k], p2[s - 1])
    acc[:, last] = y
    rows = acc.shape[0]
    tile = min(64, rows)

    @pl.loop(0, rows // tile)
    def _(i):
        part = pl.ds(pl.multiple_of(i * tile, tile), tile)
        h_val, slope = gelu_parts(acc[part, :])
        hidden[part, :] = h_val.astype(hidden.dtype)
        d_pre[part, :] = (cot[part, :].astype(jnp.float32) * slope).astype(d_pre.dtype)


def up_part(t, own, *pieces):
    _, rows, depth = t.shape
    width = own.shape[1]
    return pl.pallas_call(
        up_part_kernel,
        out_shape=jax.ShapeDtypeStruct((rows, width), jnp.float32),
        in_specs=[VMEM] * (2 + len(pieces)),
        out_specs=VMEM,
        compiler_params=params(),
        cost_estimate=cost(6 * rows * depth * width, 6 * depth * (rows + width)),
        name="up_part",
    )(t, own, *pieces)


def up_rest(t, so_far, w2, p2, cot):
    _, rows, depth = t.shape
    out = jax.ShapeDtypeStruct(cot.shape, jnp.bfloat16)
    return pl.pallas_call(
        up_rest_kernel,
        out_shape=(out, out),
        in_specs=[VMEM] * 5,
        out_specs=(VMEM, VMEM),
        scratch_shapes=[pltpu.VMEM(cot.shape, jnp.float32)],
        compiler_params=params(),
        cost_estimate=cost(2 * depth * cot.size, 2 * depth * sum(cot.shape), cot.size),
        name="up_rest",
    )(t, so_far, w2, p2, cot)


def sort_w_kernel(own, pair, x0, x1, x2, x3, y013, y2, out, sem):
    c = lax.axis_index("col")
    z = lax.axis_index("dp") & 3
    q = x0.shape[1]
    pltpu.make_async_copy(own, out.at[c], sem).start()
    pltpu.make_async_copy(pair, out.at[c ^ 1], sem).start()
    theirs = (y013.at[0], y013.at[1], y2, y013.at[2])
    for m, srcs, core in ((2, (x0, x1, x2, x3), c & 1), (3, theirs, 1 - (c & 1))):
        for u, src in enumerate(srcs):
            cols = pl.ds(pl.multiple_of(away(z, u, core) * q, 128), q)
            pltpu.make_async_copy(src, out.at[c ^ m, :, cols], sem).start()
    pltpu.make_async_copy(out, out, sem).wait()


def sort_w(*pieces):
    ff, depth = pieces[0].shape
    return pl.pallas_call(
        sort_w_kernel,
        out_shape=jax.ShapeDtypeStruct((4, ff, depth), jnp.bfloat16),
        in_specs=[ANY] * 8,
        out_specs=VMEM,
        scratch_shapes=[pltpu.SemaphoreType.DMA],
        compiler_params=params(),
        cost_estimate=cost(0, 16 * depth * ff),
        name="sort_w",
    )(*pieces)


def down_kernel(plan, w, *rest):
    r, c = lax.axis_index("row"), lax.axis_index("col")
    blocks, so_far, out = rest[: len(plan)], rest[len(plan) : -1], rest[-1]
    tile = 512

    @pl.loop(0, w.shape[2] // tile)
    def _(i):
        cols = pl.ds(pl.multiple_of(i * tile, tile), tile)
        y = so_far[0][:, cols] if so_far else None
        for s, g in zip(plan, blocks):
            part = mul(g[...], w[turned_from(away(r, s, c & 1), c), :, cols])
            y = part if y is None else y + part
        out[:, cols] = y.astype(out.dtype)


def down(w, blocks, plan, so_far, kind):
    _, ff, depth = w.shape
    rows = blocks[0].shape[0]
    more = () if so_far is None else (so_far,)
    return pl.pallas_call(
        functools.partial(down_kernel, plan),
        out_shape=jax.ShapeDtypeStruct((rows, depth), kind),
        in_specs=[VMEM] * (1 + len(blocks) + len(more)),
        out_specs=VMEM,
        compiler_params=params(),
        cost_estimate=cost(2 * len(blocks) * rows * depth * ff, 8 * ff * (rows + depth)),
        name="down",
    )(w, *blocks, *more)


def together(*xs):
    return lax.optimization_barrier(xs)


def body(tokens, w_up, cotangent):
    depth, ff = w_up.shape
    width = ff // 2
    part = depth // 4
    z = lax.axis_index("dp") % 4
    h = tokens.shape[0] // 64 * 24
    piece = lax.dynamic_slice(w_up, (z * part, width), (part, width))
    s1, s2, s3 = y_step(piece), opposite(piece), y_step(piece, 1)
    ta = col_swap(tokens[:h], 2)
    t_pair = col_swap(tokens, 1)
    p0, ta, t_pair, w0, rest, w_t = together(
        jnp.stack([s1, s2, s3]), ta, t_pair, w_up[:, :width], tokens[h:], w_up.T
    )
    p1, p3 = z_step(p0), z_step(p0, 1)
    w1, w3 = y_step(w0), y_step(w0, 1)
    tb = col_swap(rest, 2)
    p1, p3, w1, w3, ta, tb, x0 = together(
        p1, p3, w1, w3, ta, tb, lax.dynamic_slice(w_t, (0, z * part), (ff, part))
    )
    x0 = col_swap(x0, 2)
    p2 = z_step(p1)
    w2 = y_step(w1)
    t = sort_tokens(tokens, t_pair, ta, tb, col_swap(ta, 1), col_swap(tb, 1))
    so_far = up_part(t, w_up, w1, w3, p0, p1, p3)
    p2, w2, so_far, x0 = together(p2, w2, so_far, x0)
    hidden, d_pre = up_rest(t, so_far, w2, p2, cotangent)

    d_pre, x0, w_t2 = together(d_pre, x0, w_t)
    m = mirror(d_pre)
    x1, x3 = z_step(x0), z_step(x0, 1)
    w_pair = col_swap(w_t2, 1)
    m, x1, x3, w_pair = together(m, x1, x3, w_pair)
    g1, g3 = y_step(m), y_step(m, 1)
    x2 = z_step(x1)
    theirs = col_swap(jnp.stack([x0, x1, x3]), 1)
    g1, g3, x2, theirs = together(g1, g3, x2, theirs)
    g2 = y_step(g1)
    w = sort_w(w_t, w_pair, x0, x1, x2, x3, theirs, col_swap(x2, 1))
    total = down(w, (m, g1, g3), (0, 1, 3), None, jnp.float32)
    g2, total = together(g2, total)
    return hidden, down(w, (g2,), (2,), total, jnp.bfloat16)


def solution(mesh):
    placed = (P(("dp", "row"), "col"), P("row", "col"), P(("dp", "row"), "col"))
    return jax.shard_map(
        body,
        mesh=mesh,
        in_specs=placed,
        out_specs=(P(("dp", "row"), "col"), P(("dp", "col"), "row")),
        check_vma=False,
    )
```

```python
import functools
import math

import jax
import jax.numpy as jnp
from jax import lax
from jax.experimental import pallas as pl
from jax.experimental.pallas import tpu as pltpu
from jax.sharding import PartitionSpec as P

COEFF = math.sqrt(2.0 / math.pi)
MIB = 1 << 20


ANY = pl.BlockSpec(memory_space=pl.ANY)
VMEM = pl.BlockSpec(memory_space=pltpu.VMEM)


def flat(sizes, target):
    pairs = []
    for i in range(sizes[0]):
        for j in range(sizes[1]):
            a, b = target(i, j)
            pairs.append((i * sizes[1] + j, a * sizes[1] + b))
    return pairs


def y_step(x, back=0):
    sizes = (lax.axis_size("row"), lax.axis_size("col"))
    return lax.ppermute(
        x, ("row", "col"), flat(sizes, lambda r, c: ((r + 1 - 2 * ((c ^ back) & 1)) % sizes[0], c))
    )


def z_size():
    return min(8, lax.axis_size("dp"))


def z_step(x, back=0):
    sizes, n = (lax.axis_size("dp"), lax.axis_size("col")), z_size()
    return lax.ppermute(
        x, ("dp", "col"), flat(sizes, lambda i, c: (i // n * n + (i % n + 1 - 2 * ((c ^ back) & 1)) % n, c))
    )


def opposite(x):
    n = lax.axis_size("row")
    return lax.ppermute(x, "row", [(i, (i + 2) % n) for i in range(n)])


def col_swap(x, m):
    n = lax.axis_size("col")
    return lax.ppermute(x, "col", [(i, i ^ m) for i in range(n)])


def turned(r, c):
    core = c & 1
    if (c >> 1) != (r >> 1):
        step = 2 if core else 0
    else:
        step = 1 if core else -1
    return (r + step) % 4, r


def mirror(x):
    return lax.ppermute(x, ("row", "col"), flat((4, 4), turned))


def turned_from(row, col):
    step = (row - col + 4) & 3
    cross = 1 - (step & 1)
    core = jnp.where((step == 1) | (step == 2), 1, 0)
    return 2 * ((col >> 1) ^ cross) + core


def away(i, s, core):
    return (i + jnp.where(core == 0, 4 - s, s)) & 3


def gelu_parts(pre):
    sq = pre * pre
    t = jnp.tanh(COEFF * (pre + 0.044715 * sq * pre))
    hidden = 0.5 * pre * (1.0 + t)
    slope = 0.5 * (1.0 + t) + 0.5 * pre * (1.0 - t * t) * COEFF * (1.0 + 3.0 * 0.044715 * sq)
    return hidden, slope


def params():
    return pltpu.CompilerParams(vmem_limit_bytes=16 * MIB)


def cost(flops, nbytes, trans=0):
    return pl.CostEstimate(flops=flops, bytes_accessed=nbytes, transcendentals=trans)


def mul(a, b):
    return jnp.dot(a, b, preferred_element_type=jnp.float32)


def sort_tokens_kernel(t0, t1, t2, t3, out, sem):
    c = lax.axis_index("col")
    for m, src in enumerate((t0, t1, t2, t3)):
        pltpu.make_async_copy(src, out.at[c ^ m], sem).start()
    pltpu.make_async_copy(out, out, sem).wait()


def sort_tokens(*ts):
    rows, depth = ts[0].shape
    return pl.pallas_call(
        sort_tokens_kernel,
        out_shape=jax.ShapeDtypeStruct((4, rows, depth), jnp.bfloat16),
        in_specs=[ANY] * 4,
        out_specs=VMEM,
        scratch_shapes=[pltpu.SemaphoreType.DMA],
        compiler_params=params(),
        cost_estimate=cost(0, 16 * rows * depth),
        name="sort_tokens",
    )(*ts)


def up_part_kernel(t, own, w1, w3, p0, p1, p3, acc):
    r, core = lax.axis_index("row"), lax.axis_index("col") & 1
    z = lax.axis_index("dp") & 3
    _, q, width = p0.shape
    first, last = pl.ds(0, width), pl.ds(width, width)
    acc[...] = mul(t[r], own[...])
    for s, w in ((1, w1), (3, w3)):
        acc[:, first] += mul(t[away(r, s, core)], w[...])
    for s in range(1, 4):
        j = away(r, s, core)
        for u, p in ((0, p0), (1, p1), (3, p3)):
            k = pl.ds(pl.multiple_of(away(z, u, core) * q, 128), q)
            acc[:, last] += mul(t[j, :, k], p[s - 1])


def up_rest_kernel(t, so_far, w2, p2, cot, hidden, d_pre, buf, sem):
    r, core = lax.axis_index("row"), lax.axis_index("col") & 1
    z = lax.axis_index("dp") & 3
    _, q, width = p2.shape
    k = pl.ds(pl.multiple_of(away(z, 2, core) * q, 128), q)
    rows = buf.shape[0]
    tile = rows // 4
    for i in range(4):
        part = pl.ds(i * tile, tile)
        first = mul(t[away(r, 2, core), part, :], w2[...])
        last = mul(t[away(r, 1, core), part, k], p2[0])
        last += mul(t[away(r, 2, core), part, k], p2[1])
        last += mul(t[away(r, 3, core), part, k], p2[2])
        for at, y in ((0, first), (width, last)):
            cols = pl.ds(at, width)
            h_val, slope = gelu_parts(so_far[part, cols] + y)
            buf[part, cols] = h_val.astype(buf.dtype)
            d_pre[part, cols] = (cot[part, cols].astype(jnp.float32) * slope).astype(d_pre.dtype)
        pltpu.make_async_copy(buf.at[part], hidden.at[part], sem.at[i]).start()
    for i in range(4):
        part = pl.ds(i * tile, tile)
        pltpu.make_async_copy(buf.at[part], hidden.at[part], sem.at[i]).wait()


def up_part(t, own, *pieces):
    _, rows, depth = t.shape
    width = own.shape[1]
    return pl.pallas_call(
        up_part_kernel,
        out_shape=jax.ShapeDtypeStruct((rows, width), jnp.float32),
        in_specs=[VMEM] * (2 + len(pieces)),
        out_specs=VMEM,
        compiler_params=params(),
        cost_estimate=cost(6 * rows * depth * width, 6 * depth * (rows + width)),
        name="up_part",
    )(t, own, *pieces)


def up_rest(t, so_far, w2, p2, cot):
    _, rows, depth = t.shape
    out = jax.ShapeDtypeStruct(cot.shape, jnp.bfloat16)
    return pl.pallas_call(
        up_rest_kernel,
        out_shape=(out, out),
        in_specs=[VMEM] * 5,
        out_specs=(ANY, VMEM),
        scratch_shapes=[pltpu.VMEM(cot.shape, jnp.bfloat16), pltpu.SemaphoreType.DMA((4,))],
        compiler_params=params(),
        cost_estimate=cost(2 * depth * cot.size, 2 * depth * sum(cot.shape), cot.size),
        name="up_rest",
    )(t, so_far, w2, p2, cot)


def sort_w_kernel(own, pair, x0, x1, x2, x3, y0, y1, y2, y3, out, sem):
    c = lax.axis_index("col")
    z = lax.axis_index("dp") & 3
    q = x0.shape[1]
    pltpu.make_async_copy(own, out.at[c], sem).start()
    pltpu.make_async_copy(pair, out.at[c ^ 1], sem).start()
    for m, srcs, core in ((2, (x0, x1, x2, x3), c & 1), (3, (y0, y1, y2, y3), 1 - (c & 1))):
        for u, src in enumerate(srcs):
            cols = pl.ds(pl.multiple_of(away(z, u, core) * q, 128), q)
            pltpu.make_async_copy(src, out.at[c ^ m, :, cols], sem).start()
    pltpu.make_async_copy(out, out, sem).wait()


def sort_w(*pieces):
    ff, depth = pieces[0].shape
    return pl.pallas_call(
        sort_w_kernel,
        out_shape=jax.ShapeDtypeStruct((4, ff, depth), jnp.bfloat16),
        in_specs=[ANY] * 10,
        out_specs=VMEM,
        scratch_shapes=[pltpu.SemaphoreType.DMA],
        compiler_params=params(),
        cost_estimate=cost(0, 16 * depth * ff),
        name="sort_w",
    )(*pieces)


def down_kernel(plan, w, *rest):
    r, c = lax.axis_index("row"), lax.axis_index("col")
    blocks, so_far, out = rest[: len(plan)], rest[len(plan) : -1], rest[-1]
    tile = 512

    @pl.loop(0, w.shape[2] // tile)
    def _(i):
        cols = pl.ds(pl.multiple_of(i * tile, tile), tile)
        y = so_far[0][:, cols] if so_far else None
        for s, g in zip(plan, blocks):
            part = mul(g[...], w[turned_from(away(r, s, c & 1), c), :, cols])
            y = part if y is None else y + part
        out[:, cols] = y.astype(out.dtype)


def down(w, blocks, plan, so_far, kind):
    _, ff, depth = w.shape
    rows = blocks[0].shape[0]
    more = () if so_far is None else (so_far,)
    return pl.pallas_call(
        functools.partial(down_kernel, plan),
        out_shape=jax.ShapeDtypeStruct((rows, depth), kind),
        in_specs=[VMEM] * (1 + len(blocks) + len(more)),
        out_specs=VMEM,
        compiler_params=params(),
        cost_estimate=cost(2 * len(blocks) * rows * depth * ff, 8 * ff * (rows + depth)),
        name="down",
    )(w, *blocks, *more)


def down_last_kernel(w, g, so_far, out, buf, sem):
    r, c = lax.axis_index("row"), lax.axis_index("col")
    j = turned_from((r + 2) & 3, c)
    tile = buf.shape[1] // 6
    copies = []
    for i in range(6):
        cols = pl.ds(i * tile, tile)
        buf[:, cols] = (so_far[:, cols] + mul(g[...], w[j, :, cols])).astype(buf.dtype)
        copies.append(pltpu.make_async_copy(buf.at[:, cols], out.at[:, cols], sem.at[i]))
        copies[-1].start()
    for copy in copies:
        copy.wait()


def down_last(w, g, so_far):
    return pl.pallas_call(
        down_last_kernel,
        out_shape=jax.ShapeDtypeStruct(so_far.shape, jnp.bfloat16),
        in_specs=[VMEM] * 3,
        out_specs=ANY,
        scratch_shapes=[pltpu.VMEM(so_far.shape, jnp.bfloat16), pltpu.SemaphoreType.DMA((6,))],
        compiler_params=params(),
        cost_estimate=cost(2 * so_far.size * g.shape[1], 6 * so_far.size),
        name="down_last",
    )(w, g, so_far)


def together(*xs):
    return lax.optimization_barrier(xs)


def body(tokens, w_up, cotangent):
    depth, ff = w_up.shape
    width = ff // 2
    part = depth // 4
    z = lax.axis_index("dp") % 4
    piece = lax.dynamic_slice(w_up, (z * part, width), (part, width))
    s1, s2, s3 = y_step(piece), opposite(piece), y_step(piece, 1)
    t_x = col_swap(tokens, 2)
    t_pair = col_swap(tokens, 1)
    s1, s2, s3, t_pair, w0, w_t = together(s1, s2, s3, t_pair, w_up[:, :width], w_up.T)
    p0 = jnp.stack([s1, s2, s3])
    p1, p3 = z_step(p0), z_step(p0, 1)
    w1, w3 = y_step(w0), y_step(w0, 1)
    p0, p1, p3, w1, w3, t_x, x0 = together(
        p0, p1, p3, w1, w3, t_x, lax.dynamic_slice(w_t, (0, z * part), (ff, part))
    )
    x0 = col_swap(x0, 2)
    p2 = z_step(p1)
    w2 = y_step(w1)
    t = sort_tokens(tokens, t_pair, t_x, col_swap(t_x, 1))
    so_far = up_part(t, w_up, w1, w3, p0, p1, p3)
    p2, w2, so_far, x0 = together(p2, w2, so_far, x0)
    hidden, d_pre = up_rest(t, so_far, w2, p2, cotangent)

    d_pre, x0 = together(d_pre, x0)
    m = mirror(d_pre)
    x1, x3 = z_step(x0), z_step(x0, 1)
    y0 = col_swap(x0, 1)
    m, x1, x3, y0 = together(m, x1, x3, y0)
    g1, g3 = y_step(m), y_step(m, 1)
    x2 = z_step(x1)
    y1, y3 = col_swap(x1, 1), col_swap(x3, 1)
    g1, g3, x2, y1, y3, w_t2 = together(g1, g3, x2, y1, y3, w_t)
    g2 = y_step(g1)
    w = sort_w(w_t, col_swap(w_t2, 1), x0, x1, x2, x3, y0, y1, col_swap(x2, 1), y3)
    total = down(w, (m, g1, g3), (0, 1, 3), None, jnp.float32)
    g2, total = together(g2, total)
    return hidden, down_last(w, g2, total)


def solution(mesh):
    placed = (P(("dp", "row"), "col"), P("row", "col"), P(("dp", "row"), "col"))
    return jax.shard_map(
        body,
        mesh=mesh,
        in_specs=placed,
        out_specs=(P(("dp", "row"), "col"), P(("dp", "col"), "row")),
        check_vma=False,
    )
```

```python
import functools
import math

import jax
import jax.numpy as jnp
from jax import lax
from jax.experimental import pallas as pl
from jax.experimental.pallas import tpu as pltpu
from jax.sharding import PartitionSpec as P

COEFF = math.sqrt(2.0 / math.pi)
MIB = 1 << 20


ANY = pl.BlockSpec(memory_space=pl.ANY)
VMEM = pl.BlockSpec(memory_space=pltpu.VMEM)


def flat(sizes, target):
    pairs = []
    for i in range(sizes[0]):
        for j in range(sizes[1]):
            a, b = target(i, j)
            pairs.append((i * sizes[1] + j, a * sizes[1] + b))
    return pairs


def y_step(x, back=0):
    sizes = (lax.axis_size("row"), lax.axis_size("col"))
    return lax.ppermute(
        x, ("row", "col"), flat(sizes, lambda r, c: ((r + 1 - 2 * ((c ^ back) & 1)) % sizes[0], c))
    )


def z_size():
    return min(8, lax.axis_size("dp"))


def z_step(x, back=0):
    sizes, n = (lax.axis_size("dp"), lax.axis_size("col")), z_size()
    return lax.ppermute(
        x, ("dp", "col"), flat(sizes, lambda i, c: (i // n * n + (i % n + 1 - 2 * ((c ^ back) & 1)) % n, c))
    )


def opposite(x):
    n = lax.axis_size("row")
    return lax.ppermute(x, "row", [(i, (i + 2) % n) for i in range(n)])


def col_swap(x, m):
    n = lax.axis_size("col")
    return lax.ppermute(x, "col", [(i, i ^ m) for i in range(n)])


def turned(r, c):
    core = c & 1
    if (c >> 1) != (r >> 1):
        step = 2 if core else 0
    else:
        step = 1 if core else -1
    return (r + step) % 4, r


def mirror(x):
    return lax.ppermute(x, ("row", "col"), flat((4, 4), turned))


def turned_from(row, col):
    step = (row - col + 4) & 3
    cross = 1 - (step & 1)
    core = jnp.where((step == 1) | (step == 2), 1, 0)
    return 2 * ((col >> 1) ^ cross) + core


def away(i, s, core):
    return (i + jnp.where(core == 0, 4 - s, s)) & 3


def gelu_parts(pre):
    sq = pre * pre
    t = jnp.tanh(COEFF * (pre + 0.044715 * sq * pre))
    hidden = 0.5 * pre * (1.0 + t)
    slope = 0.5 * (1.0 + t) + 0.5 * pre * (1.0 - t * t) * COEFF * (1.0 + 3.0 * 0.044715 * sq)
    return hidden, slope


def params():
    return pltpu.CompilerParams(vmem_limit_bytes=16 * MIB)


def cost(flops, nbytes, trans=0):
    return pl.CostEstimate(flops=flops, bytes_accessed=nbytes, transcendentals=trans)


def mul(a, b):
    return jnp.dot(a, b, preferred_element_type=jnp.float32)


def cut_kernel(at, w, out, sem):
    rows, cols = out.shape
    z = lax.axis_index("dp") & 3
    copy = pltpu.make_async_copy(w.at[pl.ds(pl.multiple_of(z * rows, 16), rows), pl.ds(at, cols)], out, sem)
    copy.start()
    copy.wait()


def cut(w, rows, cols, at):
    return pl.pallas_call(
        functools.partial(cut_kernel, at),
        out_shape=jax.ShapeDtypeStruct((rows, cols), w.dtype),
        in_specs=[ANY],
        out_specs=VMEM,
        scratch_shapes=[pltpu.SemaphoreType.DMA],
        compiler_params=params(),
        cost_estimate=cost(0, 4 * rows * cols),
        name="cut",
    )(w)


def sort_tokens_kernel(t0, t1, t2, t3, out, sem):
    c = lax.axis_index("col")
    for m, src in enumerate((t0, t1, t2, t3)):
        pltpu.make_async_copy(src, out.at[c ^ m], sem).start()
    pltpu.make_async_copy(out, out, sem).wait()


def sort_tokens(*ts):
    rows, depth = ts[0].shape
    return pl.pallas_call(
        sort_tokens_kernel,
        out_shape=jax.ShapeDtypeStruct((4, rows, depth), jnp.bfloat16),
        in_specs=[ANY] * 4,
        out_specs=VMEM,
        scratch_shapes=[pltpu.SemaphoreType.DMA],
        compiler_params=params(),
        cost_estimate=cost(0, 16 * rows * depth),
        name="sort_tokens",
    )(*ts)


def up_part_kernel(t, own, w1, w3, p0, p1, p3, acc):
    r, core = lax.axis_index("row"), lax.axis_index("col") & 1
    z = lax.axis_index("dp") & 3
    _, q, width = p0.shape
    first, last = pl.ds(0, width), pl.ds(width, width)
    acc[...] = mul(t[r], own[...])
    for s, w in ((1, w1), (3, w3)):
        acc[:, first] += mul(t[away(r, s, core)], w[...])
    for s in range(1, 4):
        j = away(r, s, core)
        for u, p in ((0, p0), (1, p1), (3, p3)):
            k = pl.ds(pl.multiple_of(away(z, u, core) * q, 128), q)
            acc[:, last] += mul(t[j, :, k], p[s - 1])


def up_rest_kernel(t, so_far, w2, p2, cot, hidden, d_pre, buf, sem):
    r, core = lax.axis_index("row"), lax.axis_index("col") & 1
    z = lax.axis_index("dp") & 3
    _, q, width = p2.shape
    k = pl.ds(pl.multiple_of(away(z, 2, core) * q, 128), q)
    rows = buf.shape[0]
    tile = rows // 4
    for i in range(4):
        part = pl.ds(i * tile, tile)
        first = mul(t[away(r, 2, core), part, :], w2[...])
        last = mul(t[away(r, 1, core), part, k], p2[0])
        last += mul(t[away(r, 2, core), part, k], p2[1])
        last += mul(t[away(r, 3, core), part, k], p2[2])
        for at, y in ((0, first), (width, last)):
            cols = pl.ds(at, width)
            h_val, slope = gelu_parts(so_far[part, cols] + y)
            buf[part, cols] = h_val.astype(buf.dtype)
            d_pre[part, cols] = (cot[part, cols].astype(jnp.float32) * slope).astype(d_pre.dtype)
        pltpu.make_async_copy(buf.at[part], hidden.at[part], sem.at[i]).start()
    for i in range(4):
        part = pl.ds(i * tile, tile)
        pltpu.make_async_copy(buf.at[part], hidden.at[part], sem.at[i]).wait()


def up_part(t, own, *pieces):
    _, rows, depth = t.shape
    width = own.shape[1]
    return pl.pallas_call(
        up_part_kernel,
        out_shape=jax.ShapeDtypeStruct((rows, width), jnp.float32),
        in_specs=[VMEM] * (2 + len(pieces)),
        out_specs=VMEM,
        compiler_params=params(),
        cost_estimate=cost(6 * rows * depth * width, 6 * depth * (rows + width)),
        name="up_part",
    )(t, own, *pieces)


def up_rest(t, so_far, w2, p2, cot):
    _, rows, depth = t.shape
    out = jax.ShapeDtypeStruct(cot.shape, jnp.bfloat16)
    return pl.pallas_call(
        up_rest_kernel,
        out_shape=(out, out),
        in_specs=[VMEM] * 5,
        out_specs=(ANY, VMEM),
        scratch_shapes=[pltpu.VMEM(cot.shape, jnp.bfloat16), pltpu.SemaphoreType.DMA((4,))],
        compiler_params=params(),
        cost_estimate=cost(2 * depth * cot.size, 2 * depth * sum(cot.shape), cot.size),
        name="up_rest",
    )(t, so_far, w2, p2, cot)


def sort_w_kernel(own, c0, c1, c2, c3, x0, x1, x2, x3, y0, y1, y2, y3, out, sem):
    c = lax.axis_index("col")
    z = lax.axis_index("dp") & 3
    q = x0.shape[1]
    pltpu.make_async_copy(own, out.at[c], sem).start()
    h = c0.shape[0]
    for i, src in enumerate((c0, c1, c2, c3)):
        pltpu.make_async_copy(src, out.at[c ^ 1, pl.ds(i * h, h)], sem).start()
    for m, srcs, core in ((2, (x0, x1, x2, x3), c & 1), (3, (y0, y1, y2, y3), 1 - (c & 1))):
        for u, src in enumerate(srcs):
            cols = pl.ds(pl.multiple_of(away(z, u, core) * q, 128), q)
            pltpu.make_async_copy(src, out.at[c ^ m, :, cols], sem).start()
    pltpu.make_async_copy(out, out, sem).wait()


def sort_w(*pieces):
    ff, depth = pieces[0].shape
    return pl.pallas_call(
        sort_w_kernel,
        out_shape=jax.ShapeDtypeStruct((4, ff, depth), jnp.bfloat16),
        in_specs=[ANY] * 13,
        out_specs=VMEM,
        scratch_shapes=[pltpu.SemaphoreType.DMA],
        compiler_params=params(),
        cost_estimate=cost(0, 16 * depth * ff),
        name="sort_w",
    )(*pieces)


def down_kernel(plan, w, *rest):
    r, c = lax.axis_index("row"), lax.axis_index("col")
    blocks, so_far, out = rest[: len(plan)], rest[len(plan) : -1], rest[-1]
    tile = 512

    @pl.loop(0, w.shape[2] // tile)
    def _(i):
        cols = pl.ds(pl.multiple_of(i * tile, tile), tile)
        y = so_far[0][:, cols] if so_far else None
        for s, g in zip(plan, blocks):
            part = mul(g[...], w[turned_from(away(r, s, c & 1), c), :, cols])
            y = part if y is None else y + part
        out[:, cols] = y.astype(out.dtype)


def down(w, blocks, plan, so_far, kind):
    _, ff, depth = w.shape
    rows = blocks[0].shape[0]
    more = () if so_far is None else (so_far,)
    return pl.pallas_call(
        functools.partial(down_kernel, plan),
        out_shape=jax.ShapeDtypeStruct((rows, depth), kind),
        in_specs=[VMEM] * (1 + len(blocks) + len(more)),
        out_specs=VMEM,
        compiler_params=params(),
        cost_estimate=cost(2 * len(blocks) * rows * depth * ff, 8 * ff * (rows + depth)),
        name="down",
    )(w, *blocks, *more)


def down_last_kernel(w, g, so_far, out, buf, sem):
    r, c = lax.axis_index("row"), lax.axis_index("col")
    j = turned_from((r + 2) & 3, c)
    tile = buf.shape[1] // 6
    copies = []
    for i in range(6):
        cols = pl.ds(i * tile, tile)
        buf[:, cols] = (so_far[:, cols] + mul(g[...], w[j, :, cols])).astype(buf.dtype)
        copies.append(pltpu.make_async_copy(buf.at[:, cols], out.at[:, cols], sem.at[i]))
        copies[-1].start()
    for copy in copies:
        copy.wait()


def down_last(w, g, so_far):
    return pl.pallas_call(
        down_last_kernel,
        out_shape=jax.ShapeDtypeStruct(so_far.shape, jnp.bfloat16),
        in_specs=[VMEM] * 3,
        out_specs=ANY,
        scratch_shapes=[pltpu.VMEM(so_far.shape, jnp.bfloat16), pltpu.SemaphoreType.DMA((6,))],
        compiler_params=params(),
        cost_estimate=cost(2 * so_far.size * g.shape[1], 6 * so_far.size),
        name="down_last",
    )(w, g, so_far)


def together(*xs):
    return lax.optimization_barrier(xs)


def body(tokens, w_up, cotangent):
    depth, ff = w_up.shape
    width = ff // 2
    part = depth // 4
    z = lax.axis_index("dp") % 4
    piece = cut(w_up, part, width, width)
    s1, s2, s3 = y_step(piece), opposite(piece), y_step(piece, 1)
    t_x = col_swap(tokens, 2)
    t_pair = col_swap(tokens, 1)
    w_t = w_up.T
    s1, s2, s3, t_pair, w0, w_t, *quarters = together(
        s1, s2, s3, t_pair, w_up[:, :width], w_t, *jnp.split(w_t, 4)
    )
    p0 = jnp.stack([s1, s2, s3])
    p1, p3 = z_step(p0), z_step(p0, 1)
    w1, w3 = y_step(w0), y_step(w0, 1)
    p0, p1, p3, w1, w3, t_x, x0 = together(
        p0, p1, p3, w1, w3, t_x, lax.dynamic_slice(w_t, (0, z * part), (ff, part))
    )
    x0 = col_swap(x0, 2)
    p2 = z_step(p1)
    w2 = y_step(w1)
    t = sort_tokens(tokens, t_pair, t_x, col_swap(t_x, 1))
    so_far = up_part(t, w_up, w1, w3, p0, p1, p3)
    p2, w2, so_far, x0 = together(p2, w2, so_far, x0)
    hidden, d_pre = up_rest(t, so_far, w2, p2, cotangent)

    d_pre, x0, *quarters = together(d_pre, x0, *quarters)
    m = mirror(d_pre)
    x1, x3 = z_step(x0), z_step(x0, 1)
    y0, c0 = col_swap(x0, 1), col_swap(quarters[0], 1)
    m, x1, x3, y0, c0 = together(m, x1, x3, y0, c0)
    g1, g3 = y_step(m), y_step(m, 1)
    x2 = z_step(x1)
    y1, y3 = col_swap(x1, 1), col_swap(x3, 1)
    g1, g3, x2, y1, y3, *quarters = together(g1, g3, x2, y1, y3, *quarters[1:])
    g2 = y_step(g1)
    w = sort_w(w_t, c0, *[col_swap(x, 1) for x in quarters], x0, x1, x2, x3, y0, y1, col_swap(x2, 1), y3)
    total = down(w, (m, g1, g3), (0, 1, 3), None, jnp.float32)
    g2, total = together(g2, total)
    return hidden, down_last(w, g2, total)


def solution(mesh):
    placed = (P(("dp", "row"), "col"), P("row", "col"), P(("dp", "row"), "col"))
    return jax.shard_map(
        body,
        mesh=mesh,
        in_specs=placed,
        out_specs=(P(("dp", "row"), "col"), P(("dp", "col"), "row")),
        check_vma=False,
    )
```

```python
import functools
import math

import jax
import jax.numpy as jnp
from jax import lax
from jax.experimental import pallas as pl
from jax.experimental.pallas import tpu as pltpu
from jax.sharding import PartitionSpec as P

COEFF = math.sqrt(2.0 / math.pi)
MIB = 1 << 20


ANY = pl.BlockSpec(memory_space=pl.ANY)
VMEM = pl.BlockSpec(memory_space=pltpu.VMEM)


def flat(sizes, target):
    pairs = []
    for i in range(sizes[0]):
        for j in range(sizes[1]):
            a, b = target(i, j)
            pairs.append((i * sizes[1] + j, a * sizes[1] + b))
    return pairs


def y_step(x, back=0):
    sizes = (lax.axis_size("row"), lax.axis_size("col"))
    return lax.ppermute(
        x, ("row", "col"), flat(sizes, lambda r, c: ((r + 1 - 2 * ((c ^ back) & 1)) % sizes[0], c))
    )


def z_size():
    return min(8, lax.axis_size("dp"))


def z_step(x, back=0):
    sizes, n = (lax.axis_size("dp"), lax.axis_size("col")), z_size()
    return lax.ppermute(
        x, ("dp", "col"), flat(sizes, lambda i, c: (i // n * n + (i % n + 1 - 2 * ((c ^ back) & 1)) % n, c))
    )


def opposite(x):
    n = lax.axis_size("row")
    return lax.ppermute(x, "row", [(i, (i + 2) % n) for i in range(n)])


def col_swap(x, m):
    n = lax.axis_size("col")
    return lax.ppermute(x, "col", [(i, i ^ m) for i in range(n)])


def turned(r, c):
    core = c & 1
    if (c >> 1) != (r >> 1):
        step = 2 if core else 0
    else:
        step = 1 if core else -1
    return (r + step) % 4, r


def mirror(x):
    return lax.ppermute(x, ("row", "col"), flat((4, 4), turned))


def turned_from(row, col):
    step = (row - col + 4) & 3
    cross = 1 - (step & 1)
    core = jnp.where((step == 1) | (step == 2), 1, 0)
    return 2 * ((col >> 1) ^ cross) + core


def away(i, s, core):
    return (i + jnp.where(core == 0, 4 - s, s)) & 3


def gelu_parts(pre):
    sq = pre * pre
    g = 0.5 + 0.5 * jnp.tanh(pre * (COEFF + 0.044715 * COEFF * sq))
    slope = g * (1.0 + (1.0 - g) * (pre * (2.0 * COEFF + 6.0 * 0.044715 * COEFF * sq)))
    return pre * g, slope


def params():
    return pltpu.CompilerParams(vmem_limit_bytes=16 * MIB)


def cost(flops, nbytes, trans=0):
    return pl.CostEstimate(flops=flops, bytes_accessed=nbytes, transcendentals=trans)


def mul(a, b):
    return jnp.dot(a, b, preferred_element_type=jnp.float32)


def cut_kernel(at, w, out, sem):
    rows, cols = out.shape
    z = lax.axis_index("dp") & 3
    copy = pltpu.make_async_copy(w.at[pl.ds(pl.multiple_of(z * rows, 16), rows), pl.ds(at, cols)], out, sem)
    copy.start()
    copy.wait()


def cut(w, rows, cols, at):
    return pl.pallas_call(
        functools.partial(cut_kernel, at),
        out_shape=jax.ShapeDtypeStruct((rows, cols), w.dtype),
        in_specs=[ANY],
        out_specs=VMEM,
        scratch_shapes=[pltpu.SemaphoreType.DMA],
        compiler_params=params(),
        cost_estimate=cost(0, 4 * rows * cols),
        name="cut",
    )(w)


def sort_tokens_kernel(t0, t1, t2, t3, out, sem):
    c = lax.axis_index("col")
    for m, src in enumerate((t0, t1, t2, t3)):
        pltpu.make_async_copy(src, out.at[c ^ m], sem).start()
    pltpu.make_async_copy(out, out, sem).wait()


def sort_tokens(*ts):
    rows, depth = ts[0].shape
    return pl.pallas_call(
        sort_tokens_kernel,
        out_shape=jax.ShapeDtypeStruct((4, rows, depth), jnp.bfloat16),
        in_specs=[ANY] * 4,
        out_specs=VMEM,
        scratch_shapes=[pltpu.SemaphoreType.DMA],
        compiler_params=params(),
        cost_estimate=cost(0, 16 * rows * depth),
        name="sort_tokens",
    )(*ts)


def up_part_kernel(t, own, w1, w3, p0, p1, p3, acc):
    r, core = lax.axis_index("row"), lax.axis_index("col") & 1
    z = lax.axis_index("dp") & 3
    _, q, width = p0.shape
    first, last = pl.ds(0, width), pl.ds(width, width)
    acc[...] = mul(t[r], own[...])
    for s, w in ((1, w1), (3, w3)):
        acc[:, first] += mul(t[away(r, s, core)], w[...])
    for s in range(1, 4):
        j = away(r, s, core)
        for u, p in ((0, p0), (1, p1), (3, p3)):
            k = pl.ds(pl.multiple_of(away(z, u, core) * q, 128), q)
            acc[:, last] += mul(t[j, :, k], p[s - 1])


def up_rest_kernel(t, so_far, w2, p2, cot, hidden, d_pre, buf, sem):
    r, core = lax.axis_index("row"), lax.axis_index("col") & 1
    z = lax.axis_index("dp") & 3
    _, q, width = p2.shape
    k = pl.ds(pl.multiple_of(away(z, 2, core) * q, 128), q)
    rows = buf.shape[0]
    tile = rows // 4
    for i in range(4):
        part = pl.ds(i * tile, tile)
        first = mul(t[away(r, 2, core), part, :], w2[...])
        last = mul(t[away(r, 1, core), part, k], p2[0])
        last += mul(t[away(r, 2, core), part, k], p2[1])
        last += mul(t[away(r, 3, core), part, k], p2[2])
        for at, y in ((0, first), (width, last)):
            cols = pl.ds(at, width)
            h_val, slope = gelu_parts(so_far[part, cols] + y)
            buf[part, cols] = h_val.astype(buf.dtype)
            d_pre[part, cols] = (cot[part, cols].astype(jnp.float32) * slope).astype(d_pre.dtype)
        pltpu.make_async_copy(buf.at[part], hidden.at[part], sem.at[i]).start()
    for i in range(4):
        part = pl.ds(i * tile, tile)
        pltpu.make_async_copy(buf.at[part], hidden.at[part], sem.at[i]).wait()


def up_part(t, own, *pieces):
    _, rows, depth = t.shape
    width = own.shape[1]
    return pl.pallas_call(
        up_part_kernel,
        out_shape=jax.ShapeDtypeStruct((rows, width), jnp.float32),
        in_specs=[VMEM] * (2 + len(pieces)),
        out_specs=VMEM,
        compiler_params=params(),
        cost_estimate=cost(6 * rows * depth * width, 6 * depth * (rows + width)),
        name="up_part",
    )(t, own, *pieces)


def up_rest(t, so_far, w2, p2, cot):
    _, rows, depth = t.shape
    out = jax.ShapeDtypeStruct(cot.shape, jnp.bfloat16)
    return pl.pallas_call(
        up_rest_kernel,
        out_shape=(out, out),
        in_specs=[VMEM] * 5,
        out_specs=(ANY, VMEM),
        scratch_shapes=[pltpu.VMEM(cot.shape, jnp.bfloat16), pltpu.SemaphoreType.DMA((4,))],
        compiler_params=params(),
        cost_estimate=cost(2 * depth * cot.size, 2 * depth * sum(cot.shape), cot.size),
        name="up_rest",
    )(t, so_far, w2, p2, cot)


def sort_w_kernel(own, c0, c1, c2, c3, x0, x1, x2, x3, y0, y1, y2, y3, out, sem):
    c = lax.axis_index("col")
    z = lax.axis_index("dp") & 3
    q = x0.shape[1]
    pltpu.make_async_copy(own, out.at[c], sem).start()
    h = c0.shape[0]
    for i, src in enumerate((c0, c1, c2, c3)):
        pltpu.make_async_copy(src, out.at[c ^ 1, pl.ds(i * h, h)], sem).start()
    for m, srcs, core in ((2, (x0, x1, x2, x3), c & 1), (3, (y0, y1, y2, y3), 1 - (c & 1))):
        for u, src in enumerate(srcs):
            cols = pl.ds(pl.multiple_of(away(z, u, core) * q, 128), q)
            pltpu.make_async_copy(src, out.at[c ^ m, :, cols], sem).start()
    pltpu.make_async_copy(out, out, sem).wait()


def sort_w(*pieces):
    ff, depth = pieces[0].shape
    return pl.pallas_call(
        sort_w_kernel,
        out_shape=jax.ShapeDtypeStruct((4, ff, depth), jnp.bfloat16),
        in_specs=[ANY] * 13,
        out_specs=VMEM,
        scratch_shapes=[pltpu.SemaphoreType.DMA],
        compiler_params=params(),
        cost_estimate=cost(0, 16 * depth),
        name="sort_w",
    )(*pieces)


def down_kernel(plan, w, *rest):
    r, c = lax.axis_index("row"), lax.axis_index("col")
    blocks, so_far, out = rest[: len(plan)], rest[len(plan) : -1], rest[-1]
    tile = 512

    @pl.loop(0, w.shape[2] // tile)
    def _(i):
        cols = pl.ds(pl.multiple_of(i * tile, tile), tile)
        y = so_far[0][:, cols] if so_far else None
        for s, g in zip(plan, blocks):
            part = mul(g[...], w[turned_from(away(r, s, c & 1), c), :, cols])
            y = part if y is None else y + part
        out[:, cols] = y.astype(out.dtype)


def down(w, blocks, plan, so_far, kind):
    _, ff, depth = w.shape
    rows = blocks[0].shape[0]
    more = () if so_far is None else (so_far,)
    return pl.pallas_call(
        functools.partial(down_kernel, plan),
        out_shape=jax.ShapeDtypeStruct((rows, depth), kind),
        in_specs=[VMEM] * (1 + len(blocks) + len(more)),
        out_specs=VMEM,
        compiler_params=params(),
        cost_estimate=cost(2 * rows * depth, 8 * (rows + depth)),
        name="down",
    )(w, *blocks, *more)


def down_last_kernel(w, g, so_far, out, buf, sem):
    r, c = lax.axis_index("row"), lax.axis_index("col")
    j = turned_from((r + 2) & 3, c)
    tile = buf.shape[1] // 6
    copies = []
    for i in range(6):
        cols = pl.ds(i * tile, tile)
        buf[:, cols] = (so_far[:, cols] + mul(g[...], w[j, :, cols])).astype(buf.dtype)
        copies.append(pltpu.make_async_copy(buf.at[:, cols], out.at[:, cols], sem.at[i]))
        copies[-1].start()
    for copy in copies:
        copy.wait()


def down_last(w, g, so_far):
    return pl.pallas_call(
        down_last_kernel,
        out_shape=jax.ShapeDtypeStruct(so_far.shape, jnp.bfloat16),
        in_specs=[VMEM] * 3,
        out_specs=ANY,
        scratch_shapes=[pltpu.VMEM(so_far.shape, jnp.bfloat16), pltpu.SemaphoreType.DMA((6,))],
        compiler_params=params(),
        cost_estimate=cost(2 * so_far.size * g.shape[1], 6 * so_far.size),
        name="down_last",
    )(w, g, so_far)


def together(*xs):
    return lax.optimization_barrier(xs)


def body(tokens, w_up, cotangent):
    depth, ff = w_up.shape
    width = ff // 2
    part = depth // 4
    z = lax.axis_index("dp") % 4
    piece = cut(w_up, part, width, width)
    s1, s2, s3 = y_step(piece), opposite(piece), y_step(piece, 1)
    t_x = col_swap(tokens, 2)
    t_pair = col_swap(tokens, 1)
    w_t = w_up.T
    s1, s2, s3, t_pair, w0, w_t, *quarters = together(
        s1, s2, s3, t_pair, w_up[:, :width], w_t, *jnp.split(w_t, 4)
    )
    p0 = jnp.stack([s1, s2, s3])
    p1, p3 = z_step(p0), z_step(p0, 1)
    w1, w3 = y_step(w0), y_step(w0, 1)
    p0, p1, p3, w1, w3, t_x, x0 = together(
        p0, p1, p3, w1, w3, t_x, lax.dynamic_slice(w_t, (0, z * part), (ff, part))
    )
    x0 = col_swap(x0, 2)
    p2 = z_step(p1)
    w2 = y_step(w1)
    t = sort_tokens(tokens, t_pair, t_x, col_swap(t_x, 1))
    so_far = up_part(t, w_up, w1, w3, p0, p1, p3)
    p2, w2, so_far, x0 = together(p2, w2, so_far, x0)
    hidden, d_pre = up_rest(t, so_far, w2, p2, cotangent)

    d_pre, x0, *quarters = together(d_pre, x0, *quarters)
    m = mirror(d_pre)
    x1, x3 = z_step(x0), z_step(x0, 1)
    y0, c0 = col_swap(x0, 1), col_swap(quarters[0], 1)
    m, x1, x3, y0, c0 = together(m, x1, x3, y0, c0)
    g1, g3 = y_step(m), y_step(m, 1)
    x2 = z_step(x1)
    y1, y3 = col_swap(x1, 1), col_swap(x3, 1)
    g1, g3, x2, y1, y3, *quarters = together(g1, g3, x2, y1, y3, *quarters[1:])
    g2 = y_step(g1)
    w = sort_w(w_t, c0, *[col_swap(x, 1) for x in quarters], x0, x1, x2, x3, y0, y1, col_swap(x2, 1), y3)
    total = down(w, (m, g1, g3), (0, 1, 3), None, jnp.float32)
    g2, total = together(g2, total)
    return hidden, down_last(w, g2, total)


def solution(mesh):
    placed = (P(("dp", "row"), "col"), P("row", "col"), P(("dp", "row"), "col"))
    return jax.shard_map(
        body,
        mesh=mesh,
        in_specs=placed,
        out_specs=(P(("dp", "row"), "col"), P(("dp", "col"), "row")),
        check_vma=False,
    )
```

```python
import functools
import math

import jax
import jax.numpy as jnp
from jax import lax
from jax.experimental import pallas as pl
from jax.experimental.pallas import tpu as pltpu
from jax.sharding import PartitionSpec as P

COEFF = math.sqrt(2.0 / math.pi)
MIB = 1 << 20


ANY = pl.BlockSpec(memory_space=pl.ANY)
VMEM = pl.BlockSpec(memory_space=pltpu.VMEM)


def flat(sizes, target):
    pairs = []
    for i in range(sizes[0]):
        for j in range(sizes[1]):
            a, b = target(i, j)
            pairs.append((i * sizes[1] + j, a * sizes[1] + b))
    return pairs


def y_step(x, back=0):
    sizes = (lax.axis_size("row"), lax.axis_size("col"))
    return lax.ppermute(
        x, ("row", "col"), flat(sizes, lambda r, c: ((r + 1 - 2 * ((c ^ back) & 1)) % sizes[0], c))
    )


def z_size():
    return min(8, lax.axis_size("dp"))


def z_step(x, back=0):
    sizes, n = (lax.axis_size("dp"), lax.axis_size("col")), z_size()
    return lax.ppermute(
        x, ("dp", "col"), flat(sizes, lambda i, c: (i // n * n + (i % n + 1 - 2 * ((c ^ back) & 1)) % n, c))
    )


def opposite(x):
    n = lax.axis_size("row")
    return lax.ppermute(x, "row", [(i, (i + 2) % n) for i in range(n)])


def col_swap(x, m):
    n = lax.axis_size("col")
    return lax.ppermute(x, "col", [(i, i ^ m) for i in range(n)])


def turned(r, c):
    core = c & 1
    if (c >> 1) != (r >> 1):
        step = 2 if core else 0
    else:
        step = 1 if core else -1
    return (r + step) % 4, r


def mirror(x):
    return lax.ppermute(x, ("row", "col"), flat((4, 4), turned))


def turned_from(row, col):
    step = (row - col + 4) & 3
    cross = 1 - (step & 1)
    core = jnp.where((step == 1) | (step == 2), 1, 0)
    return 2 * ((col >> 1) ^ cross) + core


def away(i, s, core):
    return (i + jnp.where(core == 0, 4 - s, s)) & 3


def gelu_parts(pre):
    sq = pre * pre
    g = 0.5 + 0.5 * jnp.tanh(pre * (COEFF + 0.044715 * COEFF * sq))
    slope = g * (1.0 + (1.0 - g) * (pre * (2.0 * COEFF + 6.0 * 0.044715 * COEFF * sq)))
    return pre * g, slope


def params():
    return pltpu.CompilerParams(vmem_limit_bytes=16 * MIB)


def cost(flops, nbytes, trans=0):
    return pl.CostEstimate(flops=flops, bytes_accessed=nbytes, transcendentals=trans)


def mul(a, b):
    return jnp.dot(a, b, preferred_element_type=jnp.float32)


def cut_kernel(at, w, out, sem):
    rows, cols = out.shape
    z = lax.axis_index("dp") & 3
    copy = pltpu.make_async_copy(w.at[pl.ds(pl.multiple_of(z * rows, 16), rows), pl.ds(at, cols)], out, sem)
    copy.start()
    copy.wait()


def cut(w, rows, cols, at):
    return pl.pallas_call(
        functools.partial(cut_kernel, at),
        out_shape=jax.ShapeDtypeStruct((rows, cols), w.dtype),
        in_specs=[ANY],
        out_specs=VMEM,
        scratch_shapes=[pltpu.SemaphoreType.DMA],
        compiler_params=params(),
        cost_estimate=cost(0, 4 * rows * cols),
        name="cut",
    )(w)


def sort_tokens_kernel(t0, t1, t2, t3, out, sem):
    c = lax.axis_index("col")
    for m, src in enumerate((t0, t1, t2, t3)):
        pltpu.make_async_copy(src, out.at[c ^ m], sem).start()
    pltpu.make_async_copy(out, out, sem).wait()


def sort_tokens(*ts):
    rows, depth = ts[0].shape
    return pl.pallas_call(
        sort_tokens_kernel,
        out_shape=jax.ShapeDtypeStruct((4, rows, depth), jnp.bfloat16),
        in_specs=[ANY] * 4,
        out_specs=VMEM,
        scratch_shapes=[pltpu.SemaphoreType.DMA],
        compiler_params=params(),
        cost_estimate=cost(0, 16 * rows * depth),
        name="sort_tokens",
    )(*ts)


def up_part_kernel(t, own, w1, w3, p0, p1, p3, acc):
    r, core = lax.axis_index("row"), lax.axis_index("col") & 1
    z = lax.axis_index("dp") & 3
    _, q, width = p0.shape
    first, last = pl.ds(0, width), pl.ds(width, width)
    acc[...] = mul(t[r], own[...])
    for s, w in ((1, w1), (3, w3)):
        acc[:, first] += mul(t[away(r, s, core)], w[...])
    for s in range(1, 4):
        j = away(r, s, core)
        for u, p in ((0, p0), (1, p1), (3, p3)):
            k = pl.ds(pl.multiple_of(away(z, u, core) * q, 128), q)
            acc[:, last] += mul(t[j, :, k], p[s - 1])


def up_rest_kernel(t, so_far, w2, p2, cot, hidden, d_pre, buf, sem):
    r, core = lax.axis_index("row"), lax.axis_index("col") & 1
    z = lax.axis_index("dp") & 3
    _, q, width = p2.shape
    k = pl.ds(pl.multiple_of(away(z, 2, core) * q, 128), q)
    rows = buf.shape[0]
    tile = rows // 4
    for i in range(4):
        part = pl.ds(i * tile, tile)
        first = mul(t[away(r, 2, core), part, :], w2[...])
        last = mul(t[away(r, 1, core), part, k], p2[0])
        last += mul(t[away(r, 2, core), part, k], p2[1])
        last += mul(t[away(r, 3, core), part, k], p2[2])
        for at, y in ((0, first), (width, last)):
            cols = pl.ds(at, width)
            h_val, slope = gelu_parts(so_far[part, cols] + y)
            buf[part, cols] = h_val.astype(buf.dtype)
            d_pre[part, cols] = (cot[part, cols].astype(jnp.float32) * slope).astype(d_pre.dtype)
        pltpu.make_async_copy(buf.at[part], hidden.at[part], sem.at[i]).start()
    for i in range(4):
        part = pl.ds(i * tile, tile)
        pltpu.make_async_copy(buf.at[part], hidden.at[part], sem.at[i]).wait()


def up_part(t, own, *pieces):
    _, rows, depth = t.shape
    width = own.shape[1]
    return pl.pallas_call(
        up_part_kernel,
        out_shape=jax.ShapeDtypeStruct((rows, width), jnp.float32),
        in_specs=[VMEM] * (2 + len(pieces)),
        out_specs=VMEM,
        compiler_params=params(),
        cost_estimate=cost(6 * rows * depth * width, 6 * depth * (rows + width)),
        name="up_part",
    )(t, own, *pieces)


def up_rest(t, so_far, w2, p2, cot):
    _, rows, depth = t.shape
    out = jax.ShapeDtypeStruct(cot.shape, jnp.bfloat16)
    return pl.pallas_call(
        up_rest_kernel,
        out_shape=(out, out),
        in_specs=[VMEM] * 5,
        out_specs=(ANY, VMEM),
        scratch_shapes=[pltpu.VMEM(cot.shape, jnp.bfloat16), pltpu.SemaphoreType.DMA((4,))],
        compiler_params=params(),
        cost_estimate=cost(2 * depth * cot.size, 2 * depth * sum(cot.shape), cot.size),
        name="up_rest",
    )(t, so_far, w2, p2, cot)


def sort_w_kernel(own, c0, c1, c2, c3, x0, x1, x2, x3, y0, y1, y2, y3, out, sem):
    c = lax.axis_index("col")
    z = lax.axis_index("dp") & 3
    q = x0.shape[1]
    pltpu.make_async_copy(own, out.at[c], sem).start()
    h = c0.shape[0]
    for i, src in enumerate((c0, c1, c2, c3)):
        pltpu.make_async_copy(src, out.at[c ^ 1, pl.ds(i * h, h)], sem).start()
    for m, srcs, core in ((2, (x0, x1, x2, x3), c & 1), (3, (y0, y1, y2, y3), 1 - (c & 1))):
        for u, src in enumerate(srcs):
            cols = pl.ds(pl.multiple_of(away(z, u, core) * q, 128), q)
            pltpu.make_async_copy(src, out.at[c ^ m, :, cols], sem).start()
    pltpu.make_async_copy(out, out, sem).wait()


def sort_w(*pieces):
    ff, depth = pieces[0].shape
    return pl.pallas_call(
        sort_w_kernel,
        out_shape=jax.ShapeDtypeStruct((4, ff, depth), jnp.bfloat16),
        in_specs=[ANY] * 13,
        out_specs=VMEM,
        scratch_shapes=[pltpu.SemaphoreType.DMA],
        compiler_params=params(),
        cost_estimate=cost(0, 16 * depth),
        name="sort_w",
    )(*pieces)


def down_kernel(plan, w, *rest):
    r, c = lax.axis_index("row"), lax.axis_index("col")
    blocks, so_far, out = rest[: len(plan)], rest[len(plan) : -1], rest[-1]
    tile = 512

    @pl.loop(0, w.shape[2] // tile)
    def _(i):
        cols = pl.ds(pl.multiple_of(i * tile, tile), tile)
        y = so_far[0][:, cols] if so_far else None
        for s, g in zip(plan, blocks):
            part = mul(g[...], w[turned_from(away(r, s, c & 1), c), :, cols])
            y = part if y is None else y + part
        out[:, cols] = y.astype(out.dtype)


def down(w, blocks, plan, so_far, kind):
    _, ff, depth = w.shape
    rows = blocks[0].shape[0]
    more = () if so_far is None else (so_far,)
    return pl.pallas_call(
        functools.partial(down_kernel, plan),
        out_shape=jax.ShapeDtypeStruct((rows, depth), kind),
        in_specs=[VMEM] * (1 + len(blocks) + len(more)),
        out_specs=VMEM,
        compiler_params=params(),
        cost_estimate=cost(2 * rows * depth, 8 * (rows + depth)),
        name="down",
    )(w, *blocks, *more)


def down_last_kernel(w, g, so_far, out, buf, sem):
    r, c = lax.axis_index("row"), lax.axis_index("col")
    j = turned_from((r + 2) & 3, c)
    tile = buf.shape[1] // 3
    copies = []
    for i in range(3):
        cols = pl.ds(i * tile, tile)
        buf[:, cols] = (so_far[:, cols] + mul(g[...], w[j, :, cols])).astype(buf.dtype)
        copies.append(pltpu.make_async_copy(buf.at[:, cols], out.at[:, cols], sem.at[i]))
        copies[-1].start()
    for copy in copies:
        copy.wait()


def down_last(w, g, so_far):
    return pl.pallas_call(
        down_last_kernel,
        out_shape=jax.ShapeDtypeStruct(so_far.shape, jnp.bfloat16),
        in_specs=[VMEM] * 3,
        out_specs=ANY,
        scratch_shapes=[pltpu.VMEM(so_far.shape, jnp.bfloat16), pltpu.SemaphoreType.DMA((3,))],
        compiler_params=params(),
        cost_estimate=cost(2 * so_far.size * g.shape[1], 6 * so_far.size),
        name="down_last",
    )(w, g, so_far)


def together(*xs):
    return lax.optimization_barrier(xs)


def body(tokens, w_up, cotangent):
    depth, ff = w_up.shape
    width = ff // 2
    part = depth // 4
    z = lax.axis_index("dp") % 4
    piece = cut(w_up, part, width, width)
    s1, s2, s3 = y_step(piece), opposite(piece), y_step(piece, 1)
    t_x = col_swap(tokens, 2)
    t_pair = col_swap(tokens, 1)
    w_t = w_up.T
    s1, s2, s3, t_pair, w0, w_t, *quarters = together(
        s1, s2, s3, t_pair, w_up[:, :width], w_t, *jnp.split(w_t, 4)
    )
    p0 = jnp.stack([s1, s2, s3])
    p1, p3 = z_step(p0), z_step(p0, 1)
    w1, w3 = y_step(w0), y_step(w0, 1)
    p0, p1, p3, w1, w3, t_x, x0 = together(
        p0, p1, p3, w1, w3, t_x, lax.dynamic_slice(w_t, (0, z * part), (ff, part))
    )
    x0 = col_swap(x0, 2)
    p2 = z_step(p1)
    w2 = y_step(w1)
    t = sort_tokens(tokens, t_pair, t_x, col_swap(t_x, 1))
    so_far = up_part(t, w_up, w1, w3, p0, p1, p3)
    p2, w2, so_far = together(p2, w2, so_far)
    hidden, d_pre = up_rest(t, so_far, w2, p2, cotangent)

    d_pre, x0, *quarters = together(d_pre, x0, *quarters)
    m = mirror(d_pre)
    x1, x3 = z_step(x0), z_step(x0, 1)
    y0, c0 = col_swap(x0, 1), col_swap(quarters[0], 1)
    m, x1, x3, y0, c0 = together(m, x1, x3, y0, c0)
    g1, g3 = y_step(m), y_step(m, 1)
    x2 = z_step(x1)
    y1, y3 = col_swap(x1, 1), col_swap(x3, 1)
    g1, g3, x2, y1, y3, *quarters = together(g1, g3, x2, y1, y3, *quarters[1:])
    g2 = y_step(g1)
    w = sort_w(w_t, c0, *[col_swap(x, 1) for x in quarters], x0, x1, x2, x3, y0, y1, col_swap(x2, 1), y3)
    total = down(w, (m, g1, g3), (0, 1, 3), None, jnp.float32)
    g2, total = together(g2, total)
    return hidden, down_last(w, g2, total)


def solution(mesh):
    placed = (P(("dp", "row"), "col"), P("row", "col"), P(("dp", "row"), "col"))
    return jax.shard_map(
        body,
        mesh=mesh,
        in_specs=placed,
        out_specs=(P(("dp", "row"), "col"), P(("dp", "col"), "row")),
        check_vma=False,
    )
```

```python
import functools
import math

import jax
import jax.numpy as jnp
from jax import lax
from jax.experimental import pallas as pl
from jax.experimental.pallas import tpu as pltpu
from jax.sharding import PartitionSpec as P

COEFF = math.sqrt(2.0 / math.pi)
MIB = 1 << 20


ANY = pl.BlockSpec(memory_space=pl.ANY)
VMEM = pl.BlockSpec(memory_space=pltpu.VMEM)


def flat(sizes, target):
    pairs = []
    for i in range(sizes[0]):
        for j in range(sizes[1]):
            a, b = target(i, j)
            pairs.append((i * sizes[1] + j, a * sizes[1] + b))
    return pairs


def y_step(x, back=0):
    sizes = (lax.axis_size("row"), lax.axis_size("col"))
    return lax.ppermute(
        x, ("row", "col"), flat(sizes, lambda r, c: ((r + 1 - 2 * ((c ^ back) & 1)) % sizes[0], c))
    )


def z_size():
    return min(8, lax.axis_size("dp"))


def z_step(x, back=0):
    sizes, n = (lax.axis_size("dp"), lax.axis_size("col")), z_size()
    return lax.ppermute(
        x, ("dp", "col"), flat(sizes, lambda i, c: (i // n * n + (i % n + 1 - 2 * ((c ^ back) & 1)) % n, c))
    )


def opposite(x):
    n = lax.axis_size("row")
    return lax.ppermute(x, "row", [(i, (i + 2) % n) for i in range(n)])


def col_swap(x, m):
    n = lax.axis_size("col")
    return lax.ppermute(x, "col", [(i, i ^ m) for i in range(n)])


def turned(r, c):
    core = c & 1
    if (c >> 1) != (r >> 1):
        step = 2 if core else 0
    else:
        step = 1 if core else -1
    return (r + step) % 4, r


def mirror(x):
    return lax.ppermute(x, ("row", "col"), flat((4, 4), turned))


def turned_from(row, col):
    step = (row - col + 4) & 3
    cross = 1 - (step & 1)
    core = jnp.where((step == 1) | (step == 2), 1, 0)
    return 2 * ((col >> 1) ^ cross) + core


def away(i, s, core):
    return (i + jnp.where(core == 0, 4 - s, s)) & 3


def gelu_parts(pre):
    sq = pre * pre
    g = 0.5 + 0.5 * jnp.tanh(pre * (COEFF + 0.044715 * COEFF * sq))
    slope = g * (1.0 + (1.0 - g) * (pre * (2.0 * COEFF + 6.0 * 0.044715 * COEFF * sq)))
    return pre * g, slope


def params():
    return pltpu.CompilerParams(vmem_limit_bytes=16 * MIB)


def cost(flops, nbytes, trans=0):
    return pl.CostEstimate(flops=flops, bytes_accessed=nbytes, transcendentals=trans)


def mul(a, b):
    return jnp.dot(a, b, preferred_element_type=jnp.float32)


def cut_kernel(at, w, out, sem):
    rows, cols = out.shape
    z = lax.axis_index("dp") & 3
    copy = pltpu.make_async_copy(w.at[pl.ds(pl.multiple_of(z * rows, 16), rows), pl.ds(at, cols)], out, sem)
    copy.start()
    copy.wait()


def cut(w, rows, cols, at):
    return pl.pallas_call(
        functools.partial(cut_kernel, at),
        out_shape=jax.ShapeDtypeStruct((rows, cols), w.dtype),
        in_specs=[ANY],
        out_specs=VMEM,
        scratch_shapes=[pltpu.SemaphoreType.DMA],
        compiler_params=params(),
        cost_estimate=cost(0, 4 * rows * cols),
        name="cut",
    )(w)


def sort_tokens_kernel(t0, t1, t2, t3, out, sem):
    c = lax.axis_index("col")
    for m, src in enumerate((t0, t1, t2, t3)):
        pltpu.make_async_copy(src, out.at[c ^ m], sem).start()
    pltpu.make_async_copy(out, out, sem).wait()


def sort_tokens(*ts):
    rows, depth = ts[0].shape
    return pl.pallas_call(
        sort_tokens_kernel,
        out_shape=jax.ShapeDtypeStruct((4, rows, depth), jnp.bfloat16),
        in_specs=[ANY] * 4,
        out_specs=VMEM,
        scratch_shapes=[pltpu.SemaphoreType.DMA],
        compiler_params=params(),
        cost_estimate=cost(0, 16 * rows),
        name="sort_tokens",
    )(*ts)


def up_part_kernel(t, own, w1, w3, p0, p1, p3, acc):
    r, core = lax.axis_index("row"), lax.axis_index("col") & 1
    z = lax.axis_index("dp") & 3
    _, q, width = p0.shape
    first, last = pl.ds(0, width), pl.ds(width, width)
    acc[...] = mul(t[r], own[...])
    for s, w in ((1, w1), (3, w3)):
        acc[:, first] += mul(t[away(r, s, core)], w[...])
    for s in range(1, 4):
        j = away(r, s, core)
        for u, p in ((0, p0), (1, p1), (3, p3)):
            k = pl.ds(pl.multiple_of(away(z, u, core) * q, 128), q)
            acc[:, last] += mul(t[j, :, k], p[s - 1])


def up_rest_kernel(t, so_far, w2, p2, cot, hidden, d_pre, buf, sem):
    r, core = lax.axis_index("row"), lax.axis_index("col") & 1
    z = lax.axis_index("dp") & 3
    _, q, width = p2.shape
    k = pl.ds(pl.multiple_of(away(z, 2, core) * q, 128), q)
    rows = buf.shape[0]
    tile = rows // 4
    for i in range(4):
        part = pl.ds(i * tile, tile)
        first = mul(t[away(r, 2, core), part, :], w2[...])
        last = mul(t[away(r, 1, core), part, k], p2[0])
        last += mul(t[away(r, 2, core), part, k], p2[1])
        last += mul(t[away(r, 3, core), part, k], p2[2])
        for at, y in ((0, first), (width, last)):
            cols = pl.ds(at, width)
            h_val, slope = gelu_parts(so_far[part, cols] + y)
            buf[part, cols] = h_val.astype(buf.dtype)
            d_pre[part, cols] = (cot[part, cols].astype(jnp.float32) * slope).astype(d_pre.dtype)
        pltpu.make_async_copy(buf.at[part], hidden.at[part], sem.at[i]).start()
    for i in range(4):
        part = pl.ds(i * tile, tile)
        pltpu.make_async_copy(buf.at[part], hidden.at[part], sem.at[i]).wait()


def up_part(t, own, *pieces):
    _, rows, depth = t.shape
    width = own.shape[1]
    return pl.pallas_call(
        up_part_kernel,
        out_shape=jax.ShapeDtypeStruct((rows, width), jnp.float32),
        in_specs=[VMEM] * (2 + len(pieces)),
        out_specs=VMEM,
        compiler_params=params(),
        cost_estimate=cost(6 * rows * depth, 6 * (rows + width)),
        name="up_part",
    )(t, own, *pieces)


def up_rest(t, so_far, w2, p2, cot):
    _, rows, depth = t.shape
    out = jax.ShapeDtypeStruct(cot.shape, jnp.bfloat16)
    return pl.pallas_call(
        up_rest_kernel,
        out_shape=(out, out),
        in_specs=[VMEM] * 5,
        out_specs=(ANY, VMEM),
        scratch_shapes=[pltpu.VMEM(cot.shape, jnp.bfloat16), pltpu.SemaphoreType.DMA((4,))],
        compiler_params=params(),
        cost_estimate=cost(2 * depth * cot.size, 2 * depth * sum(cot.shape), cot.size),
        name="up_rest",
    )(t, so_far, w2, p2, cot)


def sort_w_kernel(own, c0, c1, c2, c3, x0, x1, x2, x3, y0, y1, y2, y3, out, sem):
    c = lax.axis_index("col")
    z = lax.axis_index("dp") & 3
    q = x0.shape[1]
    pltpu.make_async_copy(own, out.at[c], sem).start()
    h = c0.shape[0]
    for i, src in enumerate((c0, c1, c2, c3)):
        pltpu.make_async_copy(src, out.at[c ^ 1, pl.ds(i * h, h)], sem).start()
    for m, srcs, core in ((2, (x0, x1, x2, x3), c & 1), (3, (y0, y1, y2, y3), 1 - (c & 1))):
        for u, src in enumerate(srcs):
            cols = pl.ds(pl.multiple_of(away(z, u, core) * q, 128), q)
            pltpu.make_async_copy(src, out.at[c ^ m, :, cols], sem).start()
    pltpu.make_async_copy(out, out, sem).wait()


def sort_w(*pieces):
    ff, depth = pieces[0].shape
    return pl.pallas_call(
        sort_w_kernel,
        out_shape=jax.ShapeDtypeStruct((4, ff, depth), jnp.bfloat16),
        in_specs=[ANY] * 13,
        out_specs=VMEM,
        scratch_shapes=[pltpu.SemaphoreType.DMA],
        compiler_params=params(),
        cost_estimate=cost(0, 16 * depth),
        name="sort_w",
    )(*pieces)


def down_kernel(plan, w, *rest):
    r, c = lax.axis_index("row"), lax.axis_index("col")
    blocks, so_far, out = rest[: len(plan)], rest[len(plan) : -1], rest[-1]
    tile = 512

    @pl.loop(0, w.shape[2] // tile)
    def _(i):
        cols = pl.ds(pl.multiple_of(i * tile, tile), tile)
        y = so_far[0][:, cols] if so_far else None
        for s, g in zip(plan, blocks):
            part = mul(g[...], w[turned_from(away(r, s, c & 1), c), :, cols])
            y = part if y is None else y + part
        out[:, cols] = y.astype(out.dtype)


def down(w, blocks, plan, so_far, kind):
    _, ff, depth = w.shape
    rows = blocks[0].shape[0]
    more = () if so_far is None else (so_far,)
    return pl.pallas_call(
        functools.partial(down_kernel, plan),
        out_shape=jax.ShapeDtypeStruct((rows, depth), kind),
        in_specs=[VMEM] * (1 + len(blocks) + len(more)),
        out_specs=VMEM,
        compiler_params=params(),
        cost_estimate=cost(2 * rows * depth, 8 * (rows + depth)),
        name="down",
    )(w, *blocks, *more)


def down_last_kernel(w, g, so_far, out, buf, sem):
    r, c = lax.axis_index("row"), lax.axis_index("col")
    j = turned_from((r + 2) & 3, c)
    tile = buf.shape[1] // 3
    copies = []
    for i in range(3):
        cols = pl.ds(i * tile, tile)
        buf[:, cols] = (so_far[:, cols] + mul(g[...], w[j, :, cols])).astype(buf.dtype)
        copies.append(pltpu.make_async_copy(buf.at[:, cols], out.at[:, cols], sem.at[i]))
        copies[-1].start()
    for copy in copies:
        copy.wait()


def down_last(w, g, so_far):
    return pl.pallas_call(
        down_last_kernel,
        out_shape=jax.ShapeDtypeStruct(so_far.shape, jnp.bfloat16),
        in_specs=[VMEM] * 3,
        out_specs=ANY,
        scratch_shapes=[pltpu.VMEM(so_far.shape, jnp.bfloat16), pltpu.SemaphoreType.DMA((3,))],
        compiler_params=params(),
        cost_estimate=cost(2 * so_far.size * g.shape[1], 6 * so_far.size),
        name="down_last",
    )(w, g, so_far)


def together(*xs):
    return lax.optimization_barrier(xs)


def body(tokens, w_up, cotangent):
    depth, ff = w_up.shape
    width = ff // 2
    part = depth // 4
    z = lax.axis_index("dp") % 4
    piece = cut(w_up, part, width, width)
    s1, s2, s3 = y_step(piece), opposite(piece), y_step(piece, 1)
    t_x = col_swap(tokens, 2)
    t_pair = col_swap(tokens, 1)
    w_t = w_up.T
    s1, s2, s3, t_pair, w0, w_t, *quarters = together(
        s1, s2, s3, t_pair, w_up[:, :width], w_t, *jnp.split(w_t, 4)
    )
    p0 = jnp.stack([s1, s2, s3])
    p1, p3 = z_step(p0), z_step(p0, 1)
    w1, w3 = y_step(w0), y_step(w0, 1)
    p0, p1, p3, w1, w3, t_x, x0 = together(
        p0, p1, p3, w1, w3, t_x, lax.dynamic_slice(w_t, (0, z * part), (ff, part))
    )
    x0 = col_swap(x0, 2)
    p2 = z_step(p1)
    w2 = y_step(w1)
    t = sort_tokens(tokens, t_pair, t_x, col_swap(t_x, 1))
    so_far = up_part(t, w_up, w1, w3, p0, p1, p3)
    p2, w2, so_far = together(p2, w2, so_far)
    hidden, d_pre = up_rest(t, so_far, w2, p2, cotangent)

    d_pre, x0, *quarters = together(d_pre, x0, *quarters)
    m = mirror(d_pre)
    x1, x3 = z_step(x0), z_step(x0, 1)
    y0, c0 = col_swap(x0, 1), col_swap(quarters[0], 1)
    m, x1, x3, y0, c0 = together(m, x1, x3, y0, c0)
    g1, g3 = y_step(m), y_step(m, 1)
    x2 = z_step(x1)
    y1, y3 = col_swap(x1, 1), col_swap(x3, 1)
    g1, g3, x2, y1, y3, *quarters = together(g1, g3, x2, y1, y3, *quarters[1:])
    g2 = y_step(g1)
    w = sort_w(w_t, c0, *[col_swap(x, 1) for x in quarters], x0, x1, x2, x3, y0, y1, col_swap(x2, 1), y3)
    total = down(w, (m, g1, g3), (0, 1, 3), None, jnp.float32)
    g2, total = together(g2, total)
    return hidden, down_last(w, g2, total)


def solution(mesh):
    placed = (P(("dp", "row"), "col"), P("row", "col"), P(("dp", "row"), "col"))
    return jax.shard_map(
        body,
        mesh=mesh,
        in_specs=placed,
        out_specs=(P(("dp", "row"), "col"), P(("dp", "col"), "row")),
        check_vma=False,
    )
```
